32 devices in a mesh: sim: 2 (over y), band: 4 (over z), ord: 4 (over x, core).
Axes of the slice: x: 2, y: 2, z: 4, core: 2. Of those that a mesh axis runs over, the one named last changes fastest.
Arguments:
- alm: bfloat16 [12, 256, 8192], P('sim', 'ord', 'band'), parts along dimension 0, may hold values from -6 to 6
- legendre: bfloat16 [16, 256, 8192], P(None, 'ord', 'band'), may hold values from -0.005859375 to 0.005859375
- order_ids: int32 [256], P('ord'), may hold values from 0 to 8191, as said below
- cycle_number: int32 [16], P('band'), may hold values from 1 to 32767
- src_band: int32 [4096, 1], P(('sim', 'band', 'ord')), parts along dimension 0, may hold values from 0 to 3; in each aligned block of 128 rows (0 to 127, 128 to 255, ...) at most 64 rows name the same one
- src_block: int32 [4096], P(('sim', 'band', 'ord')), parts along dimension 0, may hold values from 0 to 127
- weights: bfloat16 [4096, 128, 128], P(('sim', 'band', 'ord')), parts along dimension 0, may hold values from -0.5 to 0.5
Outputs:
- sky_map: bfloat16 [6, 16, 16384], P('sim', 'band', 'ord'), parts along dimension 0
- lensed: float32 [6, 16, 16384], P('sim', 'band', 'ord'), parts along dimension 0
The draws below stay inside these ranges and needn't reach their ends.
There are 2 independent parts, one for each index of `sim`. The reference program is written for one: setup_inputs(seed, part) draws one part's arguments, and reference() takes and returns one part's arrays. A program takes and returns all parts, laid end to end along the dimension named above; an argument that names none is the same for every part. Nothing has to cross between parts.
Inputs may be any that keep to these rules, and one draw needn't show every extreme that they name: `src_band`: among the blocks of one device at most 64 name the same band, a bound that some block reaches. `order_ids`: distinct values; one of them is 0.
All inputs are finite; a program needn't handle non-finite values.
Results may differ from the reference program's by a relative error of at most 0.0029.
Values may be sent and summed in bfloat16 or wider, within the bound.
A program may use at most 128 MiB of HBM per device.

```python
import math
import jax
import jax.numpy as jnp
import numpy as np
from jax import lax

L = 8192
NPIX = 16384
BLK = 128
CYCLE_DEV = 4
CYCLES = 16
MO = 256
NB_DEV = 128
CAP = 64
N_BAND = 4
N_ORD = 4


def draw_order_ids(key, part):
    others = jax.random.permutation(jax.random.fold_in(key, 11), NPIX // 2 - 1)[:MO].astype(jnp.int32) + 1
    zero_slot = jax.random.randint(jax.random.fold_in(key, 23), (), 0, MO).astype(jnp.int32)
    return others.at[zero_slot].set(0).astype(jnp.int32)


def with_ends(array, own_key, smallest, top_value):
    longest = array.shape.index(max(array.shape))
    spots = []
    for shift in (0, 1):
        where = [jax.random.randint(jax.random.fold_in(own_key, axis), (), 0, length) for axis, length in enumerate(array.shape)]
        where[longest] = (where[longest] + shift) % array.shape[longest]
        spots.append(tuple(where))
    return array.at[spots[0]].set(smallest).at[spots[1]].set(top_value)


def strengthened(array, key, source, target, blocks, factor):
    def block_of(dim):
        return (jnp.arange(array.shape[dim]) // (array.shape[dim] // blocks)).reshape((-1,) + (1,) * (array.ndim - 1 - dim))

    first = jax.random.permutation(key, blocks)[block_of(target)]
    other_side = (block_of(target) + blocks // 2) % blocks
    return jnp.where((block_of(source) == first) | (block_of(source) == other_side), factor * array, array)


def levels(key, extent, pieces, low, top_value):
    gain, own = 1.0, jax.random.fold_in(key, 6)
    for position, blocks in pieces:
        heights = jnp.exp(jax.random.uniform(jax.random.fold_in(own, position), (blocks,), jnp.float32, low / len(pieces), top_value / len(pieces)))
        gain = gain * jnp.repeat(heights, extent[position] // blocks).reshape([-1 if axis == position else 1 for axis in range(len(extent))])
    return gain


def assign_block(stream_key, own, number, rows, number_of, top, bound, slope):
    order = jax.random.permutation(stream_key, number_of)
    heavy_load, usual = portions_of(number_of, rows * top, bound, slope, True), portions_of(number_of, rows * top, bound, slope, False)
    places = jnp.arange(number_of)

    def named(lengths, offset_by):
        used = int((lengths > 0).sum())
        fixed = max(1, used // 4)
        passed = fixed + (places - fixed + offset_by * (used - fixed)) % max(1, number_of - fixed)
        return jnp.zeros((number_of,), jnp.int32).at[order[jnp.where(places < fixed, places, passed)]].set(jnp.asarray(lengths, jnp.int32))

    lengths = jnp.where(number % 4 == 0, named(heavy_load, number // 4), named(usual, number - number // 4 - 1))
    mixed = jax.random.permutation(jax.random.fold_in(own, 3), number_of)
    giver, receiver = mixed[0:number_of // 2 * 2:2], mixed[1:number_of // 2 * 2:2]
    slack = jnp.minimum(lengths[giver] - 1, bound - lengths[receiver]) // 2
    slack = jnp.where((giver == order[0]) | (receiver == order[0]) | (lengths[receiver] == 0), 0, jnp.maximum(slack, 0))
    passed = jax.random.randint(jax.random.fold_in(own, 4), (number_of // 2,), 0, 1 << 20) % (slack + 1)
    lengths = lengths.at[giver].add(-passed).at[receiver].add(passed)
    labels = jnp.searchsorted(jnp.cumsum(lengths), jnp.arange(rows * top), side="right").astype(jnp.int32)
    listing = labels.reshape(top, rows).T
    listing = listing[jax.random.permutation(jax.random.fold_in(own, 1), rows)]
    offset_by = jax.random.randint(jax.random.fold_in(own, 2), (rows, 1), 0, top)
    return jnp.take_along_axis(listing, (jnp.arange(top)[None, :] + offset_by) % top, axis=1)


def portions_of(number_of, total, limit, slope, full):
    loads = [(1 << 20) // math.isqrt(standing ** slope) + 1 for standing in range(1, number_of + 1)]
    largest = limit if full else min(limit, max(-(-total // number_of), total * loads[0] // sum(loads)))
    least = 1 if total - largest >= number_of - 1 else 0
    holding, rest = [largest] + [least] * (number_of - 1), total - largest - least * (number_of - 1)
    while rest > 0:
        candidates = [i for i in range(1, number_of) if holding[i] < largest] or [i for i in range(1, number_of) if holding[i] < limit]
        pool, remaining = sum([loads[i] for i in candidates]), rest
        for i in candidates:
            extra = min(limit - holding[i], max(1, remaining * loads[i] // pool), rest)
            holding[i] = holding[i] + extra
            rest = rest - extra
    return np.array(holding)


def centred(key, shape, deviation, most, shards=(), kind=jnp.bfloat16):
    values = deviation * jax.random.normal(key, shape, jnp.float32)
    if shards:
        values = values * levels(key, shape, shards, -0.22, 0.18)
    return jnp.clip(values, -most, most).astype(kind)


def heavy_noise(rng, shape, spread, bound, split, heavy, held_as=jnp.bfloat16):
    values = spread * jax.random.normal(rng, shape, jnp.float32)
    if split:
        values = values * levels(rng, shape, split, -0.22, 0.18)
    return jnp.clip(strengthened(values, jax.random.fold_in(rng, 3), *heavy), -bound, bound).astype(held_as)


def setup_inputs(seed: int = 0, part: int = 0) -> dict:
    key_of = jax.random.split(jax.random.key(seed), 8)
    part_splits = jax.random.split(jax.random.fold_in(key_of[7], part), 8)
    alm = centred(part_splits[0], (6, MO, L), 1.0, 6.0, ((1, 4), (2, 4)))
    legendre = heavy_noise(key_of[1], (CYCLES, MO, L), (L * MO) ** -0.5, 0.005859375, ((1, 4), (2, 4)), (2, 0, 4, 2.0))
    order_ids = draw_order_ids(jax.random.fold_in(key_of[7], 71), part)
    cycle_number = with_ends(jax.random.randint(key_of[3], (CYCLES,), 1, 2 * NPIX), jax.random.fold_in(key_of[3], 1), 1, (2 * NPIX) - 1).astype(jnp.int32)
    src_band_keys = jax.random.split(jax.random.fold_in(part_splits[4], 1), (NB_DEV * N_BAND * N_ORD) // NB_DEV)
    src_band_turns = jax.random.permutation(jax.random.fold_in(part_splits[4], 3), (NB_DEV * N_BAND * N_ORD) // NB_DEV)
    src_band = jax.vmap(lambda own, number: assign_block(jax.random.fold_in(part_splits[4], 2), own, number, NB_DEV, N_BAND, 1, CAP, 2))(src_band_keys, src_band_turns).reshape((NB_DEV * N_BAND * N_ORD, 1))
    src_block = with_ends(jax.random.randint(part_splits[5], (NB_DEV * N_BAND * N_ORD,), 0, NB_DEV), jax.random.fold_in(part_splits[5], 1), 0, NB_DEV - 1).astype(jnp.int32)
    weights = centred(part_splits[6], (NB_DEV * N_BAND * N_ORD, BLK, BLK), BLK ** -0.5, 0.5, ((0, 16),))
    return dict(alm=alm, legendre=legendre, order_ids=order_ids, cycle_number=cycle_number, src_band=src_band, src_block=src_block, weights=weights)


def rotate(coeffs, order_ids, cycle_number):
    parity = (cycle_number % 2).astype(jnp.float32)
    orders = order_ids.astype(jnp.float32)
    angle = (math.pi / NPIX) * orders[None, :] * parity[:, None]
    cosine = jnp.cos(angle)[:, None, :]
    sine = jnp.sin(angle)[:, None, :]
    factor = jnp.where(order_ids == 0, 1.0, 2.0).astype(jnp.float32)[None, None, :]
    real_part = coeffs[:, 0:3, :]
    imag_part = coeffs[:, 3:6, :]
    rot_re = factor * (real_part * cosine - imag_part * sine)
    rot_im = factor * (real_part * sine + imag_part * cosine)
    return rot_re, rot_im


def synthesize(rot_re, rot_im, order_ids, columns):
    phase = (order_ids[:, None] * columns[None, :]) % NPIX
    angle = phase.astype(jnp.float32) * (2.0 * math.pi / NPIX)
    right = jnp.concatenate([jnp.cos(angle), jnp.sin(angle)], axis=0)
    cycles = rot_re.shape[0]
    left = jnp.concatenate([rot_re, -rot_im], axis=2).reshape(cycles * 3, -1)
    pixels = jnp.dot(left, right, precision=lax.Precision.HIGHEST, preferred_element_type=jnp.float32)
    return jnp.transpose(pixels.reshape(cycles, 3, -1), (1, 0, 2))


def reference(alm, legendre, order_ids, cycle_number, src_band, src_block, weights):
    def one_order(index):
        rows = lax.dynamic_index_in_dim(legendre, index, 1, keepdims=False)
        terms = lax.dynamic_index_in_dim(alm, index, 1, keepdims=False)
        return jnp.dot(rows, terms.T, preferred_element_type=jnp.float32)

    per_order = lax.map(one_order, jnp.arange(MO, dtype=jnp.int32))
    coeffs = jnp.transpose(per_order, (1, 2, 0))
    rot_re, rot_im = rotate(coeffs, order_ids, cycle_number)
    columns = jnp.arange(NPIX, dtype=jnp.int32)
    sky_map = synthesize(rot_re, rot_im, order_ids, columns).astype(jnp.bfloat16)
    npix_here = NPIX // N_ORD
    blocks = sky_map.reshape(3, N_BAND, CYCLE_DEV, N_ORD, npix_here)
    blocks = jnp.transpose(blocks, (0, 1, 3, 2, 4)).reshape(3, N_BAND, N_ORD, NB_DEV, BLK)
    source_band = src_band[:, 0].reshape(N_BAND, N_ORD, NB_DEV)
    source_index = src_block.reshape(N_BAND, N_ORD, NB_DEV)
    ord_index = jnp.arange(N_ORD, dtype=jnp.int32)[None, :, None]
    source = blocks[:, source_band, ord_index, source_index, :]
    source = jnp.transpose(source, (1, 2, 0, 3, 4)).reshape(N_BAND * N_ORD, 3, NB_DEV, BLK)
    matrices = weights.reshape(N_BAND * N_ORD, NB_DEV, BLK, BLK)

    def one_device(pair):
        mats, values = pair
        return jnp.einsum("kij,ckj->cki", mats.astype(jnp.float32), values.astype(jnp.float32))

    lensed = lax.map(one_device, (matrices, source))
    lensed = lensed.reshape(N_BAND, N_ORD, 3, CYCLE_DEV, npix_here)
    lensed = jnp.transpose(lensed, (2, 0, 3, 1, 4)).reshape(3, N_BAND * CYCLE_DEV, NPIX)
    return sky_map, lensed
```

```python
import functools
import math

import jax
import jax.numpy as jnp
from jax import lax
from jax.experimental import pallas as pl
from jax.experimental.pallas import tpu as pltpu
from jax.sharding import PartitionSpec as P

BLK = 128
MESH = pl.DeviceIdType.MESH
SUB = 16
WIDE = 256
CHUNKS = 4


def cosine(phase, period):
    half, quarter = period // 2, period // 4
    centred = ((phase + half) & (period - 1)) - half
    x = (quarter - jnp.abs(centred)).astype(jnp.float32) * (2.0 * math.pi / period)
    y = x * x
    tail = -1.0 / 39916800 * y + 1.0 / 362880
    tail = tail * y - 1.0 / 5040
    tail = tail * y + 1.0 / 120
    tail = tail * y - 1.0 / 6
    return x + x * y * tail


def exchange(bands, ords, cyc, npix, cycle_ref, order_ref, alm_ref, leg_ref, out_ref,
             alm_buf, leg_buf, part, landed, mine, gathered,
             alm_sem, leg_sem, rs_send, rs_recv, ag_send, ag_recv):
    b, o = lax.axis_index("band"), lax.axis_index("ord")
    devices = bands * ords
    me = b * ords + o
    chunks = alm_buf.shape[0]
    cycles = leg_buf.shape[1]
    rows = part.shape[1]
    half = chunks * SUB

    def fetch_alm(q):
        return pltpu.make_async_copy(
            alm_ref.at[:, pl.ds(q * SUB, SUB), :], alm_buf.at[q, pl.ds(0, 6)], alm_sem.at[q])

    def fetch_leg(q):
        return pltpu.make_async_copy(
            leg_ref.at[:, pl.ds(q * SUB, SUB), :], leg_buf.at[q], leg_sem.at[q])

    for q in range(chunks):
        fetch_alm(q).start()
        fetch_leg(q).start()

    barrier = pltpu.get_barrier_semaphore()

    def greet(t, _):
        to = lax.rem(me + t, devices)
        pl.semaphore_signal(barrier, inc=1, device_id={"band": to // ords, "ord": lax.rem(to, ords)},
                            device_id_type=MESH)
        return 0

    lax.fori_loop(1, devices, greet, 0)

    near = lax.broadcasted_iota(jnp.int32, (1, SUB, BLK), 1)
    far = lax.broadcasted_iota(jnp.int32, (1, SUB, BLK), 2) % SUB
    keep = near == far
    lane = lax.broadcasted_iota(jnp.int32, (cycles, BLK), 1)
    packed = [jnp.zeros((cycles, BLK), jnp.float32) for _ in range(3)]
    for q in range(chunks):
        alm_buf[q, 6:8] = jnp.zeros((2, SUB, alm_buf.shape[3]), jnp.bfloat16)
        fetch_alm(q).wait()
        fetch_leg(q).wait()
        depth = alm_buf.shape[3]
        product = lax.dot_general(
            leg_buf[q].reshape(cycles * SUB, depth), alm_buf[q].reshape(8 * SUB, depth),
            (((1,), (1,)), ((), ())), preferred_element_type=jnp.float32)
        diag = jnp.sum(jnp.where(keep, product.reshape(cycles, SUB, BLK), 0.0), axis=1)
        for f in range(3):
            for side in range(2):
                start = side * half + q * SUB
                shift = (start - (f + 3 * side) * SUB) % BLK
                moved = pltpu.roll(diag, shift, 1) if shift else diag
                packed[f] = jnp.where((lane >= start) & (lane < start + SUB), moved, packed[f])
    part[:, 3 * cyc:rows, :] = jnp.zeros((bands, rows - 3 * cyc, BLK), jnp.float32)
    for f in range(3):
        for d in range(bands):
            part[d, f * cyc:(f + 1) * cyc, :] = packed[f][d * cyc:(d + 1) * cyc]

    pl.semaphore_wait(barrier, devices - 1)

    def scatter(t):
        to = lax.rem(b + t, bands)
        return pltpu.make_async_remote_copy(
            src_ref=part.at[to], dst_ref=landed.at[t], send_sem=rs_send.at[t], recv_sem=rs_recv.at[t],
            device_id={"band": to}, device_id_type=MESH)

    def begin(make):
        def step(t, _):
            make(t).start()
            return 0
        return step

    def ended(make):
        def step(t, _):
            make(t).wait()
            return 0
        return step

    lax.fori_loop(1, bands, begin(scatter), 0)

    m = order_ref[...]
    row = lax.broadcasted_iota(jnp.int32, (rows, BLK), 0)
    side = lax.broadcasted_iota(jnp.int32, (rows, BLK), 1) // half
    parity = jnp.zeros((rows, BLK), jnp.int32)
    for r in range(cyc):
        parity = jnp.where(row % cyc == r, cycle_ref[r] & 1, parity)
    angle = m * parity
    cos_a = cosine(angle, 2 * npix)
    sin_a = cosine(angle + jnp.where(side == 0, npix // 2, npix // 2 * 3), 2 * npix)
    factor = jnp.where(m == 0, 1.0, 2.0)

    lax.fori_loop(1, bands, ended(scatter), 0)

    total = lax.fori_loop(1, bands, lambda t, acc: acc + landed[t], part[b])
    turned = factor * (total * cos_a + pltpu.roll(total, half, 1) * sin_a)
    turned = jnp.where(row == 3 * cyc, m.astype(jnp.float32), turned)
    mine[...] = turned

    def spread(t):
        to = lax.rem(me + t, devices)
        return pltpu.make_async_remote_copy(
            src_ref=mine, dst_ref=gathered.at[t], send_sem=ag_send.at[t], recv_sem=ag_recv.at[t],
            device_id={"band": to // ords, "ord": lax.rem(to, ords)}, device_id_type=MESH)

    lax.fori_loop(1, devices, begin(spread), 0)
    out_ref[me] = turned
    lax.fori_loop(1, devices, ended(spread), 0)

    def place(t, _):
        out_ref[lax.rem(me - t + devices, devices)] = gathered[t]
        return 0

    lax.fori_loop(1, devices, place, 0)


def lens(bands, ords, cyc, npix, where_ref, band_ref, block_ref, coef_ref, weights_ref, sky_ref, lensed_ref,
         high, low, table, picked, weights_buf, sem):
    b, o = where_ref[0], where_ref[1]
    here = npix // ords
    groups = here // WIDE
    depth = ords * BLK
    count = weights_buf.shape[0]
    slab = count // CHUNKS
    lines = bands * 3 * cyc
    halves = WIDE // BLK
    per_cycle = here // BLK

    def fetch(c):
        return pltpu.make_async_copy(
            weights_ref.at[pl.ds(c * slab, slab)], weights_buf.at[pl.ds(c * slab, slab)], sem.at[c])

    for c in range(CHUNKS):
        fetch(c).start()

    m = jnp.concatenate([coef_ref[k, 3 * cyc:3 * cyc + 1, :] for k in range(ords)], axis=1).astype(jnp.int32)

    def lanes(count_rows):
        side = (lax.broadcasted_iota(jnp.int32, (count_rows, depth), 1) // (BLK // 2)) % 2
        return lax.broadcasted_iota(jnp.int32, (count_rows, depth), 0), side

    pixel, side = lanes(WIDE)
    waves = cosine(m * pixel + side * (npix // 4), npix)
    waves_high = waves.astype(jnp.bfloat16)
    waves_low = (waves - waves_high.astype(jnp.float32)).astype(jnp.bfloat16)
    group, side = lanes(groups)
    start = m * (o * here + group * WIDE)
    cos_g = cosine(start, npix)
    sin_g = cosine(start + jnp.where(side == 0, npix // 4, npix // 4 * 3), npix)

    for d in range(bands):
        plain = jnp.concatenate([coef_ref[d * ords + k, 0:3 * cyc, :] for k in range(ords)], axis=1)
        swapped = jnp.concatenate(
            [pltpu.roll(coef_ref[d * ords + k], BLK // 2, 1)[0:3 * cyc] for k in range(ords)], axis=1)
        for g in range(groups):
            value = plain * cos_g[g:g + 1] + swapped * sin_g[g:g + 1]
            upper = value.astype(jnp.bfloat16).astype(jnp.float32)
            at = g * lines + d * 3 * cyc
            high[at:at + 3 * cyc, :] = upper
            low[at:at + 3 * cyc, :] = value - upper

    span = min(lines * groups, 768)
    for s in range(0, lines * groups, span):
        left_high = high[s:s + span, :].astype(jnp.bfloat16)
        left_low = low[s:s + span, :].astype(jnp.bfloat16)

        def times(left, right):
            return lax.dot_general(left, right, (((1,), (1,)), ((), ())), preferred_element_type=jnp.float32)

        pixels = times(left_high, waves_high) + (times(left_high, waves_low) + times(left_low, waves_high))
        pixels = pixels.astype(jnp.bfloat16).astype(jnp.float32)
        for h in range(halves):
            table[h, s:s + span, :] = pixels[:, h * BLK:(h + 1) * BLK]

    for g in range(groups):
        for h in range(halves):
            for f in range(3):
                value = table[h, pl.ds(g * lines + b * (3 * cyc) + f * cyc, cyc), :]
                at = g * WIDE + h * BLK
                sky_ref[f, :, at:at + BLK] = value.astype(jnp.bfloat16)

    for c in range(CHUNKS):
        fetch(c).wait()

    def pick(p, _):
        for r in range(cyc):
            n = r * per_cycle + p
            block = block_ref[n]
            cycle, spot = block // per_cycle, block % per_cycle
            line = (spot // halves) * lines + band_ref[n] * (3 * cyc) + cycle
            for f in range(3):
                picked[n, pl.ds(f, 1), :] = table[spot % halves, pl.ds(line + f * cyc, 1), :]
        return 0

    lax.fori_loop(0, per_cycle, pick, 0, unroll=2)

    def apply(p, _):
        for r in range(cyc):
            n = r * per_cycle + p
            made = lax.dot_general(
                picked[n].astype(jnp.bfloat16), weights_buf[n], (((1,), (1,)), ((), ())),
                preferred_element_type=jnp.float32)
            for f in range(3):
                lensed_ref[f, r:r + 1, pl.ds(pl.multiple_of(p * BLK, BLK), BLK)] = made[f:f + 1]
        return 0

    lax.fori_loop(0, per_cycle, apply, 0, unroll=4)


def local(bands, ords, npix, alm, legendre, order_ids, cycle_number, src_band, src_block, weights):
    cyc = cycle_number.shape[0]
    orders = order_ids.shape[0]
    depth = alm.shape[2]
    cycles = legendre.shape[0]
    chunks = orders // SUB
    rows = -(-(3 * cyc + 1) // 8) * 8
    devices = bands * ords
    here = npix // ords
    vmem = pl.BlockSpec(memory_space=pltpu.VMEM)
    smem = pl.BlockSpec(memory_space=pltpu.SMEM)
    anywhere = pl.BlockSpec(memory_space=pl.ANY)
    doubled = jnp.concatenate([order_ids, order_ids]).reshape(1, 2 * orders)
    coef = pl.pallas_call(
        functools.partial(exchange, bands, ords, cyc, npix),
        out_shape=jax.ShapeDtypeStruct((devices, rows, BLK), jnp.float32),
        in_specs=[smem, vmem, anywhere, anywhere],
        out_specs=vmem,
        scratch_shapes=[
            pltpu.VMEM((chunks, 8, SUB, depth), jnp.bfloat16),
            pltpu.VMEM((chunks, cycles, SUB, depth), jnp.bfloat16),
            pltpu.VMEM((bands, rows, BLK), jnp.float32),
            pltpu.VMEM((bands, rows, BLK), jnp.float32),
            pltpu.VMEM((rows, BLK), jnp.float32),
            pltpu.VMEM((devices, rows, BLK), jnp.float32),
            pltpu.SemaphoreType.DMA((chunks,)),
            pltpu.SemaphoreType.DMA((chunks,)),
            pltpu.SemaphoreType.DMA((bands,)),
            pltpu.SemaphoreType.DMA((bands,)),
            pltpu.SemaphoreType.DMA((devices,)),
            pltpu.SemaphoreType.DMA((devices,)),
        ],
        compiler_params=pltpu.CompilerParams(
            collective_id=0, has_side_effects=True, vmem_limit_bytes=24 * 2**20),
        name="exchange",
    )(cycle_number, doubled, alm, legendre)
    place = jnp.stack([lax.axis_index("band"), lax.axis_index("ord")]).astype(jnp.int32)
    lines = bands * 3 * cyc * (here // WIDE)
    count = weights.shape[0]
    return pl.pallas_call(
        functools.partial(lens, bands, ords, cyc, npix),
        out_shape=(
            jax.ShapeDtypeStruct((3, cyc, here), jnp.bfloat16),
            jax.ShapeDtypeStruct((3, cyc, here), jnp.float32),
        ),
        in_specs=[smem, smem, smem, vmem, anywhere],
        out_specs=(vmem, vmem),
        scratch_shapes=[
            pltpu.VMEM((lines, ords * BLK), jnp.float32),
            pltpu.VMEM((lines, ords * BLK), jnp.float32),
            pltpu.VMEM((WIDE // BLK, lines, BLK), jnp.float32),
            pltpu.VMEM((count, 8, BLK), jnp.float32),
            pltpu.VMEM(weights.shape, jnp.bfloat16),
            pltpu.SemaphoreType.DMA((CHUNKS,)),
        ],
        compiler_params=pltpu.CompilerParams(vmem_limit_bytes=48 * 2**20),
        name="lens",
    )(place, src_band.reshape(count), src_block, coef, weights)


def solution(mesh):
    placed = (
        P("sim", "ord", "band"),
        P(None, "ord", "band"),
        P("ord"),
        P("band"),
        P(("sim", "band", "ord"), None),
        P(("sim", "band", "ord")),
        P(("sim", "band", "ord"), None, None),
    )

    def whole(alm, legendre, order_ids, cycle_number, src_band, src_block, weights):
        blocks = weights.shape[0] // mesh.shape["sim"]
        npix = blocks * weights.shape[2] // cycle_number.shape[0]
        return jax.shard_map(
            functools.partial(local, mesh.shape["band"], mesh.shape["ord"], npix),
            mesh=mesh,
            in_specs=placed,
            out_specs=(P("sim", "band", "ord"), P("sim", "band", "ord")),
            check_vma=False,
        )(alm, legendre, order_ids, cycle_number, src_band, src_block, weights)

    return whole
```

```python
import functools
import math

import jax
import jax.numpy as jnp
from jax import lax
from jax.experimental import pallas as pl
from jax.experimental.pallas import tpu as pltpu
from jax.sharding import PartitionSpec as P

BLK = 128
MESH = pl.DeviceIdType.MESH
SUB = 16
WIDE = 256
CHUNKS = 4


def cosine(phase, period):
    half, quarter = period // 2, period // 4
    centred = ((phase + half) & (period - 1)) - half
    x = (quarter - jnp.abs(centred)).astype(jnp.float32) * (2.0 * math.pi / period)
    y = x * x
    tail = -1.0 / 39916800 * y + 1.0 / 362880
    tail = tail * y - 1.0 / 5040
    tail = tail * y + 1.0 / 120
    tail = tail * y - 1.0 / 6
    return x + x * y * tail


def loop(first, last, step):
    return lax.fori_loop(first, last, step, 0, unroll=True if last <= 16 else 1)


def exchange(bands, ords, cyc, npix, cycle_ref, order_ref, alm_ref, leg_ref, out_ref,
             alm_buf, leg_buf, part, landed, mine, gathered,
             alm_sem, leg_sem, rs_send, rs_recv, ag_send, ag_recv):
    b, o = lax.axis_index("band"), lax.axis_index("ord")
    devices = bands * ords
    me = b * ords + o
    chunks = alm_buf.shape[0]
    cycles = leg_buf.shape[1]
    rows = part.shape[1]
    half = chunks * SUB

    def fetch_alm(q):
        return pltpu.make_async_copy(
            alm_ref.at[:, pl.ds(q * SUB, SUB), :], alm_buf.at[q, pl.ds(0, 6)], alm_sem.at[q])

    def fetch_leg(q):
        return pltpu.make_async_copy(
            leg_ref.at[:, pl.ds(q * SUB, SUB), :], leg_buf.at[q], leg_sem.at[q])

    for q in range(chunks):
        fetch_alm(q).start()
        fetch_leg(q).start()

    barrier = pltpu.get_barrier_semaphore()

    def greet(t, _):
        to = lax.rem(me + t, devices)
        pl.semaphore_signal(barrier, inc=1, device_id={"band": to // ords, "ord": lax.rem(to, ords)},
                            device_id_type=MESH)
        return 0

    loop(1, devices, greet)

    near = lax.broadcasted_iota(jnp.int32, (1, SUB, BLK), 1)
    far = lax.broadcasted_iota(jnp.int32, (1, SUB, BLK), 2) % SUB
    keep = near == far
    lane = lax.broadcasted_iota(jnp.int32, (cycles, BLK), 1)
    packed = [jnp.zeros((cycles, BLK), jnp.float32) for _ in range(3)]
    for q in range(chunks):
        alm_buf[q, 6:8] = jnp.zeros((2, SUB, alm_buf.shape[3]), jnp.bfloat16)
        fetch_alm(q).wait()
        fetch_leg(q).wait()
        depth = alm_buf.shape[3]
        product = lax.dot_general(
            leg_buf[q].reshape(cycles * SUB, depth), alm_buf[q].reshape(8 * SUB, depth),
            (((1,), (1,)), ((), ())), preferred_element_type=jnp.float32)
        diag = jnp.sum(jnp.where(keep, product.reshape(cycles, SUB, BLK), 0.0), axis=1)
        for f in range(3):
            for side in range(2):
                start = side * half + q * SUB
                shift = (start - (f + 3 * side) * SUB) % BLK
                moved = pltpu.roll(diag, shift, 1) if shift else diag
                packed[f] = jnp.where((lane >= start) & (lane < start + SUB), moved, packed[f])
    part[:, 3 * cyc:rows, :] = jnp.zeros((bands, rows - 3 * cyc, BLK), jnp.float32)
    for f in range(3):
        for d in range(bands):
            part[d, f * cyc:(f + 1) * cyc, :] = packed[f][d * cyc:(d + 1) * cyc]

    pl.semaphore_wait(barrier, devices - 1)

    def scatter(t):
        to = lax.rem(b + t, bands)
        return pltpu.make_async_remote_copy(
            src_ref=part.at[to], dst_ref=landed.at[t], send_sem=rs_send.at[t], recv_sem=rs_recv.at[t],
            device_id={"band": to}, device_id_type=MESH)

    def begin(make):
        def step(t, _):
            make(t).start()
            return 0
        return step

    def ended(make):
        def step(t, _):
            make(t).wait()
            return 0
        return step

    loop(1, bands, begin(scatter))

    m = jnp.concatenate([order_ref[...], order_ref[...]], axis=1)
    row = lax.broadcasted_iota(jnp.int32, (rows, BLK), 0)
    side = lax.broadcasted_iota(jnp.int32, (rows, BLK), 1) // half
    parity = jnp.zeros((rows, BLK), jnp.int32)
    for r in range(cyc):
        parity = jnp.where(row % cyc == r, cycle_ref[r] & 1, parity)
    angle = m * parity
    cos_a = cosine(angle, 2 * npix)
    sin_a = cosine(angle + jnp.where(side == 0, npix // 2, npix // 2 * 3), 2 * npix)
    factor = jnp.where(m == 0, 1.0, 2.0)

    loop(1, bands, ended(scatter))

    total = lax.fori_loop(1, bands, lambda t, acc: acc + landed[t], part[b])
    turned = factor * (total * cos_a + pltpu.roll(total, half, 1) * sin_a)
    turned = jnp.where(row == 3 * cyc, m.astype(jnp.float32), turned)
    mine[...] = turned

    def spread(t):
        to = lax.rem(me + t, devices)
        return pltpu.make_async_remote_copy(
            src_ref=mine, dst_ref=gathered.at[t], send_sem=ag_send.at[t], recv_sem=ag_recv.at[t],
            device_id={"band": to // ords, "ord": lax.rem(to, ords)}, device_id_type=MESH)

    loop(1, devices, begin(spread))
    out_ref[me] = turned
    loop(1, devices, ended(spread))

    def place(t, _):
        out_ref[lax.rem(me - t + devices, devices)] = gathered[t]
        return 0

    loop(1, devices, place)


def lens(bands, ords, cyc, npix, band_ref, block_ref, coef_ref, weights_ref, sky_ref, lensed_ref,
         high, low, table, picked, weights_buf, sem):
    b, o = lax.axis_index("band"), lax.axis_index("ord")
    here = npix // ords
    groups = here // WIDE
    depth = ords * BLK
    count = weights_buf.shape[0]
    slab = count // CHUNKS
    lines = bands * 3 * cyc
    halves = WIDE // BLK
    per_cycle = here // BLK

    def fetch(c):
        return pltpu.make_async_copy(
            weights_ref.at[pl.ds(c * slab, slab)], weights_buf.at[pl.ds(c * slab, slab)], sem.at[c])

    for c in range(CHUNKS):
        fetch(c).start()

    m = jnp.concatenate([coef_ref[k, 3 * cyc:3 * cyc + 1, :] for k in range(ords)], axis=1).astype(jnp.int32)

    def lanes(count_rows):
        side = (lax.broadcasted_iota(jnp.int32, (count_rows, depth), 1) // (BLK // 2)) % 2
        return lax.broadcasted_iota(jnp.int32, (count_rows, depth), 0), side

    pixel, side = lanes(WIDE)
    waves = cosine(m * pixel + side * (npix // 4), npix)
    waves_high = waves.astype(jnp.bfloat16)
    waves_low = (waves - waves_high.astype(jnp.float32)).astype(jnp.bfloat16)
    group, side = lanes(groups)
    start = m * (o * here + group * WIDE)
    cos_g = cosine(start, npix)
    sin_g = cosine(start + jnp.where(side == 0, npix // 4, npix // 4 * 3), npix)

    for d in range(bands):
        plain = jnp.concatenate([coef_ref[d * ords + k, 0:3 * cyc, :] for k in range(ords)], axis=1)
        swapped = jnp.concatenate(
            [pltpu.roll(coef_ref[d * ords + k], BLK // 2, 1)[0:3 * cyc] for k in range(ords)], axis=1)
        for g in range(groups):
            value = plain * cos_g[g:g + 1] + swapped * sin_g[g:g + 1]
            upper = value.astype(jnp.bfloat16).astype(jnp.float32)
            at = g * lines + d * 3 * cyc
            high[at:at + 3 * cyc, :] = upper
            low[at:at + 3 * cyc, :] = value - upper

    span = min(lines * groups, 768)
    for s in range(0, lines * groups, span):
        left_high = high[s:s + span, :].astype(jnp.bfloat16)
        left_low = low[s:s + span, :].astype(jnp.bfloat16)

        def times(left, right):
            return lax.dot_general(left, right, (((1,), (1,)), ((), ())), preferred_element_type=jnp.float32)

        pixels = times(left_high, waves_high) + (times(left_high, waves_low) + times(left_low, waves_high))
        pixels = pixels.astype(jnp.bfloat16).astype(jnp.float32)
        for h in range(halves):
            table[h, s:s + span, :] = pixels[:, h * BLK:(h + 1) * BLK]

    for g in range(groups):
        for h in range(halves):
            for f in range(3):
                value = table[h, pl.ds(g * lines + b * (3 * cyc) + f * cyc, cyc), :]
                at = g * WIDE + h * BLK
                sky_ref[f, :, at:at + BLK] = value.astype(jnp.bfloat16)

    many = BLK // (4 * cyc)
    groups_out = per_cycle // many
    picked[...] = jnp.zeros(picked.shape, jnp.float32)

    def pick(p, _):
        for r in range(cyc):
            n = r * per_cycle + p
            block = block_ref[n]
            cycle, spot = block // per_cycle, block % per_cycle
            line = (spot // halves) * lines + band_ref[n] * (3 * cyc) + cycle
            for f in range(3):
                at = f * (many * cyc) + (p % many) * cyc + r
                picked[p // many, pl.ds(at, 1), :] = table[spot % halves, pl.ds(line + f * cyc, 1), :]
        return 0

    lax.fori_loop(0, per_cycle, pick, 0, unroll=4)

    for c in range(CHUNKS):
        fetch(c).wait()

    odd = lax.broadcasted_iota(jnp.int32, (BLK, BLK), 0) % 2
    spot_of = lax.broadcasted_iota(jnp.int32, (BLK, BLK), 1) % (many * cyc) // 2

    def apply(k, _):
        source = picked[k]
        right = jnp.concatenate(
            [jnp.where(odd == 0, source, 0.0), jnp.where(odd == 1, source, 0.0)], axis=1).astype(jnp.bfloat16)
        made = jnp.zeros((BLK, BLK), jnp.float32)
        for p in range(many):
            for r in range(0, cyc, 2):
                n = r * per_cycle + k * many + p
                left = jnp.concatenate([weights_buf[n], weights_buf[n + per_cycle]], axis=1)
                product = lax.dot_general(
                    left, right, (((1,), (1,)), ((), ())), preferred_element_type=jnp.float32)
                made = jnp.where(spot_of == (p * cyc + r) // 2, product, made)
        made = made.T
        for p in range(many):
            for f in range(3):
                at = f * (many * cyc) + p * cyc
                lanes_at = pl.ds(pl.multiple_of((k * many + p) * BLK, BLK), BLK)
                lensed_ref[f, :, lanes_at] = made[at:at + cyc]
        return 0

    lax.fori_loop(0, groups_out, apply, 0, unroll=2)


def local(bands, ords, npix, alm, legendre, order_ids, cycle_number, src_band, src_block, weights):
    cyc = cycle_number.shape[0]
    orders = order_ids.shape[0]
    depth = alm.shape[2]
    cycles = legendre.shape[0]
    chunks = orders // SUB
    rows = -(-(3 * cyc + 1) // 8) * 8
    devices = bands * ords
    here = npix // ords
    vmem = pl.BlockSpec(memory_space=pltpu.VMEM)
    smem = pl.BlockSpec(memory_space=pltpu.SMEM)
    anywhere = pl.BlockSpec(memory_space=pl.ANY)
    coef = pl.pallas_call(
        functools.partial(exchange, bands, ords, cyc, npix),
        out_shape=jax.ShapeDtypeStruct((devices, rows, BLK), jnp.float32),
        in_specs=[smem, vmem, anywhere, anywhere],
        out_specs=vmem,
        scratch_shapes=[
            pltpu.VMEM((chunks, 8, SUB, depth), jnp.bfloat16),
            pltpu.VMEM((chunks, cycles, SUB, depth), jnp.bfloat16),
            pltpu.VMEM((bands, rows, BLK), jnp.float32),
            pltpu.VMEM((bands, rows, BLK), jnp.float32),
            pltpu.VMEM((rows, BLK), jnp.float32),
            pltpu.VMEM((devices, rows, BLK), jnp.float32),
            pltpu.SemaphoreType.DMA((chunks,)),
            pltpu.SemaphoreType.DMA((chunks,)),
            pltpu.SemaphoreType.DMA((bands,)),
            pltpu.SemaphoreType.DMA((bands,)),
            pltpu.SemaphoreType.DMA((devices,)),
            pltpu.SemaphoreType.DMA((devices,)),
        ],
        compiler_params=pltpu.CompilerParams(
            collective_id=0, has_side_effects=True, vmem_limit_bytes=60 * 2**20),
        name="exchange",
    )(cycle_number, order_ids.reshape(1, orders), alm, legendre)
    lines = bands * 3 * cyc * (here // WIDE)
    count = weights.shape[0]
    return pl.pallas_call(
        functools.partial(lens, bands, ords, cyc, npix),
        out_shape=(
            jax.ShapeDtypeStruct((3, cyc, here), jnp.bfloat16),
            jax.ShapeDtypeStruct((3, cyc, here), jnp.float32),
        ),
        in_specs=[smem, smem, vmem, anywhere],
        out_specs=(vmem, vmem),
        scratch_shapes=[
            pltpu.VMEM((lines, ords * BLK), jnp.float32),
            pltpu.VMEM((lines, ords * BLK), jnp.float32),
            pltpu.VMEM((WIDE // BLK, lines, BLK), jnp.float32),
            pltpu.VMEM((count * 4 // BLK, BLK, BLK), jnp.float32),
            pltpu.VMEM(weights.shape, jnp.bfloat16),
            pltpu.SemaphoreType.DMA((CHUNKS,)),
        ],
        compiler_params=pltpu.CompilerParams(vmem_limit_bytes=60 * 2**20),
        name="lens",
    )(src_band.reshape(count), src_block, coef, weights)


def solution(mesh):
    placed = (
        P("sim", "ord", "band"),
        P(None, "ord", "band"),
        P("ord"),
        P("band"),
        P(("sim", "band", "ord"), None),
        P(("sim", "band", "ord")),
        P(("sim", "band", "ord"), None, None),
    )

    def whole(alm, legendre, order_ids, cycle_number, src_band, src_block, weights):
        blocks = weights.shape[0] // mesh.shape["sim"]
        npix = blocks * weights.shape[2] // cycle_number.shape[0]
        return jax.shard_map(
            functools.partial(local, mesh.shape["band"], mesh.shape["ord"], npix),
            mesh=mesh,
            in_specs=placed,
            out_specs=(P("sim", "band", "ord"), P("sim", "band", "ord")),
            check_vma=False,
        )(alm, legendre, order_ids, cycle_number, src_band, src_block, weights)

    return whole
```

```python
import functools
import math

import jax
import jax.numpy as jnp
from jax import lax
from jax.experimental import pallas as pl
from jax.experimental.pallas import tpu as pltpu
from jax.sharding import PartitionSpec as P

BLK = 128
MESH = pl.DeviceIdType.MESH
SUB = 16
WIDE = 256
CHUNKS = 4


def cosine(phase, period):
    half, quarter = period // 2, period // 4
    centred = ((phase + half) & (period - 1)) - half
    x = (quarter - jnp.abs(centred)).astype(jnp.float32) * (2.0 * math.pi / period)
    y = x * x
    tail = -1.0 / 39916800 * y + 1.0 / 362880
    tail = tail * y - 1.0 / 5040
    tail = tail * y + 1.0 / 120
    tail = tail * y - 1.0 / 6
    return x + x * y * tail


def loop(first, last, step):
    return lax.fori_loop(first, last, step, 0, unroll=True if last <= 16 else 1)


def exchange(bands, ords, cyc, npix, cycle_ref, order_ref, alm_ref, leg_ref, out_ref,
             alm_buf, leg_buf, part, landed, mine, gathered,
             alm_sem, leg_sem, rs_send, rs_recv, ag_send, ag_recv):
    b, o = lax.axis_index("band"), lax.axis_index("ord")
    devices = bands * ords
    me = b * ords + o
    chunks = alm_buf.shape[0]
    cycles = leg_buf.shape[1]
    rows = part.shape[1]
    half = chunks * SUB

    def fetch_alm(q):
        return pltpu.make_async_copy(
            alm_ref.at[:, pl.ds(q * SUB, SUB), :], alm_buf.at[q, pl.ds(0, 6)], alm_sem.at[q])

    def fetch_leg(q):
        return pltpu.make_async_copy(
            leg_ref.at[:, pl.ds(q * SUB, SUB), :], leg_buf.at[q], leg_sem.at[q])

    for q in range(chunks):
        fetch_alm(q).start()
        fetch_leg(q).start()

    barrier = pltpu.get_barrier_semaphore()

    def greet(t, _):
        to = lax.rem(me + t, devices)
        pl.semaphore_signal(barrier, inc=1, device_id={"band": to // ords, "ord": lax.rem(to, ords)},
                            device_id_type=MESH)
        return 0

    loop(1, devices, greet)

    near = lax.broadcasted_iota(jnp.int32, (1, SUB, BLK), 1)
    far = lax.broadcasted_iota(jnp.int32, (1, SUB, BLK), 2) % SUB
    keep = near == far
    lane = lax.broadcasted_iota(jnp.int32, (cycles, BLK), 1)
    packed = [jnp.zeros((cycles, BLK), jnp.float32) for _ in range(3)]
    for q in range(chunks):
        alm_buf[q, 6:8] = jnp.zeros((2, SUB, alm_buf.shape[3]), jnp.bfloat16)
        fetch_alm(q).wait()
        fetch_leg(q).wait()
        depth = alm_buf.shape[3]
        product = lax.dot_general(
            leg_buf[q].reshape(cycles * SUB, depth), alm_buf[q].reshape(8 * SUB, depth),
            (((1,), (1,)), ((), ())), preferred_element_type=jnp.float32)
        diag = jnp.sum(jnp.where(keep, product.reshape(cycles, SUB, BLK), 0.0), axis=1)
        for f in range(3):
            for side in range(2):
                start = side * half + q * SUB
                shift = (start - (f + 3 * side) * SUB) % BLK
                moved = pltpu.roll(diag, shift, 1) if shift else diag
                packed[f] = jnp.where((lane >= start) & (lane < start + SUB), moved, packed[f])
    part[:, 3 * cyc:rows, :] = jnp.zeros((bands, rows - 3 * cyc, BLK), jnp.float32)
    for f in range(3):
        for d in range(bands):
            part[d, f * cyc:(f + 1) * cyc, :] = packed[f][d * cyc:(d + 1) * cyc]

    pl.semaphore_wait(barrier, devices - 1)

    def scatter(t):
        to = lax.rem(b + t, bands)
        return pltpu.make_async_remote_copy(
            src_ref=part.at[to], dst_ref=landed.at[t], send_sem=rs_send.at[t], recv_sem=rs_recv.at[t],
            device_id={"band": to}, device_id_type=MESH)

    def begin(make):
        def step(t, _):
            make(t).start()
            return 0
        return step

    def ended(make):
        def step(t, _):
            make(t).wait()
            return 0
        return step

    loop(1, bands, begin(scatter))

    m = jnp.concatenate([order_ref[...], order_ref[...]], axis=1)
    row = lax.broadcasted_iota(jnp.int32, (rows, BLK), 0)
    side = lax.broadcasted_iota(jnp.int32, (rows, BLK), 1) // half
    parity = jnp.zeros((rows, BLK), jnp.int32)
    for r in range(cyc):
        parity = jnp.where(row % cyc == r, cycle_ref[r] & 1, parity)
    angle = m * parity
    cos_a = cosine(angle, 2 * npix)
    sin_a = cosine(angle + jnp.where(side == 0, npix // 2, npix // 2 * 3), 2 * npix)
    factor = jnp.where(m == 0, 1.0, 2.0)

    loop(1, bands, ended(scatter))

    total = lax.fori_loop(1, bands, lambda t, acc: acc + landed[t], part[b])
    turned = factor * (total * cos_a + pltpu.roll(total, half, 1) * sin_a)
    turned = jnp.where(row == 3 * cyc, m.astype(jnp.float32), turned)
    mine[...] = turned

    def spread(t):
        to = lax.rem(me + t, devices)
        return pltpu.make_async_remote_copy(
            src_ref=mine, dst_ref=gathered.at[t], send_sem=ag_send.at[t], recv_sem=ag_recv.at[t],
            device_id={"band": to // ords, "ord": lax.rem(to, ords)}, device_id_type=MESH)

    loop(1, devices, begin(spread))
    out_ref[me] = turned
    loop(1, devices, ended(spread))

    def place(t, _):
        out_ref[lax.rem(me - t + devices, devices)] = gathered[t]
        return 0

    loop(1, devices, place)


def lens(bands, ords, cyc, npix, band_ref, block_ref, coef_ref, weights_ref, sky_ref, lensed_ref,
         high, low, table, picked, weights_buf, sem):
    b, o = lax.axis_index("band"), lax.axis_index("ord")
    here = npix // ords
    groups = here // WIDE
    depth = ords * BLK
    count = weights_buf.shape[0]
    slab = count // CHUNKS
    lines = bands * 3 * cyc
    halves = WIDE // BLK
    per_cycle = here // BLK

    def fetch(c):
        return pltpu.make_async_copy(
            weights_ref.at[pl.ds(c * slab, slab)], weights_buf.at[pl.ds(c * slab, slab)], sem.at[c])

    for c in range(CHUNKS):
        fetch(c).start()

    m = jnp.concatenate([coef_ref[k, 3 * cyc:3 * cyc + 1, :] for k in range(ords)], axis=1).astype(jnp.int32)

    def lanes(count_rows):
        side = (lax.broadcasted_iota(jnp.int32, (count_rows, depth), 1) // (BLK // 2)) % 2
        return lax.broadcasted_iota(jnp.int32, (count_rows, depth), 0), side

    pixel, side = lanes(WIDE)
    waves = cosine(m * pixel + side * (npix // 4), npix)
    waves_high = waves.astype(jnp.bfloat16)
    waves_low = (waves - waves_high.astype(jnp.float32)).astype(jnp.bfloat16)
    group, side = lanes(groups)
    start = m * (o * here + group * WIDE)
    cos_g = cosine(start, npix)
    sin_g = cosine(start + jnp.where(side == 0, npix // 4, npix // 4 * 3), npix)

    for d in range(bands):
        plain = jnp.concatenate([coef_ref[d * ords + k, 0:3 * cyc, :] for k in range(ords)], axis=1)
        swapped = jnp.concatenate(
            [pltpu.roll(coef_ref[d * ords + k], BLK // 2, 1)[0:3 * cyc] for k in range(ords)], axis=1)
        for g in range(groups):
            value = plain * cos_g[g:g + 1] + swapped * sin_g[g:g + 1]
            upper = value.astype(jnp.bfloat16).astype(jnp.float32)
            at = g * lines + d * 3 * cyc
            high[at:at + 3 * cyc, :] = upper
            low[at:at + 3 * cyc, :] = value - upper

    span = min(lines * groups, 768)
    for s in range(0, lines * groups, span):
        left_high = high[s:s + span, :].astype(jnp.bfloat16)
        left_low = low[s:s + span, :].astype(jnp.bfloat16)

        def times(left, right):
            return lax.dot_general(left, right, (((1,), (1,)), ((), ())), preferred_element_type=jnp.float32)

        pixels = times(left_high, waves_high) + (times(left_high, waves_low) + times(left_low, waves_high))
        pixels = pixels.astype(jnp.bfloat16).astype(jnp.float32)
        for h in range(halves):
            table[h, s:s + span, :] = pixels[:, h * BLK:(h + 1) * BLK]

    for g in range(groups):
        for h in range(halves):
            for f in range(3):
                value = table[h, pl.ds(g * lines + b * (3 * cyc) + f * cyc, cyc), :]
                at = g * WIDE + h * BLK
                sky_ref[f, :, at:at + BLK] = value.astype(jnp.bfloat16)

    many = BLK // (4 * cyc)
    groups_out = per_cycle // many
    picked[...] = jnp.zeros(picked.shape, jnp.float32)

    def pick(p, _):
        for r in range(cyc):
            n = r * per_cycle + p
            block = block_ref[n]
            cycle, spot = block // per_cycle, block % per_cycle
            line = (spot // halves) * lines + band_ref[n] * (3 * cyc) + cycle
            for f in range(3):
                at = f * (many * cyc) + (p % many) * cyc + r
                picked[p // many, pl.ds(at, 1), :] = table[spot % halves, pl.ds(line + f * cyc, 1), :]
        return 0

    lax.fori_loop(0, per_cycle, pick, 0, unroll=2)

    for c in range(CHUNKS):
        fetch(c).wait()

    odd = lax.broadcasted_iota(jnp.int32, (BLK, BLK), 0) % 2
    spot_of = lax.broadcasted_iota(jnp.int32, (BLK, BLK), 1) % (many * cyc) // 2

    def apply(k, _):
        source = picked[k]
        right = jnp.concatenate(
            [jnp.where(odd == 0, source, 0.0), jnp.where(odd == 1, source, 0.0)], axis=1).astype(jnp.bfloat16)
        made = jnp.zeros((BLK, BLK), jnp.float32)
        for p in range(many):
            for r in range(0, cyc, 2):
                n = r * per_cycle + k * many + p
                left = jnp.concatenate([weights_buf[n], weights_buf[n + per_cycle]], axis=1)
                product = lax.dot_general(
                    left, right, (((1,), (1,)), ((), ())), preferred_element_type=jnp.float32)
                made = jnp.where(spot_of == (p * cyc + r) // 2, product, made)
        made = made.T
        for p in range(many):
            for f in range(3):
                at = f * (many * cyc) + p * cyc
                lanes_at = pl.ds(pl.multiple_of((k * many + p) * BLK, BLK), BLK)
                lensed_ref[f, :, lanes_at] = made[at:at + cyc]
        return 0

    lax.fori_loop(0, groups_out, apply, 0)


def local(bands, ords, npix, alm, legendre, order_ids, cycle_number, src_band, src_block, weights):
    cyc = cycle_number.shape[0]
    orders = order_ids.shape[0]
    depth = alm.shape[2]
    cycles = legendre.shape[0]
    chunks = orders // SUB
    rows = -(-(3 * cyc + 1) // 8) * 8
    devices = bands * ords
    here = npix // ords
    vmem = pl.BlockSpec(memory_space=pltpu.VMEM)
    smem = pl.BlockSpec(memory_space=pltpu.SMEM)
    anywhere = pl.BlockSpec(memory_space=pl.ANY)
    coef = pl.pallas_call(
        functools.partial(exchange, bands, ords, cyc, npix),
        out_shape=jax.ShapeDtypeStruct((devices, rows, BLK), jnp.float32),
        in_specs=[smem, vmem, anywhere, anywhere],
        out_specs=vmem,
        scratch_shapes=[
            pltpu.VMEM((chunks, 8, SUB, depth), jnp.bfloat16),
            pltpu.VMEM((chunks, cycles, SUB, depth), jnp.bfloat16),
            pltpu.VMEM((bands, rows, BLK), jnp.float32),
            pltpu.VMEM((bands, rows, BLK), jnp.float32),
            pltpu.VMEM((rows, BLK), jnp.float32),
            pltpu.VMEM((devices, rows, BLK), jnp.float32),
            pltpu.SemaphoreType.DMA((chunks,)),
            pltpu.SemaphoreType.DMA((chunks,)),
            pltpu.SemaphoreType.DMA((bands,)),
            pltpu.SemaphoreType.DMA((bands,)),
            pltpu.SemaphoreType.DMA((devices,)),
            pltpu.SemaphoreType.DMA((devices,)),
        ],
        compiler_params=pltpu.CompilerParams(
            collective_id=0, has_side_effects=True, vmem_limit_bytes=60 * 2**20),
        name="exchange",
    )(cycle_number, order_ids.reshape(1, orders), alm, legendre)
    lines = bands * 3 * cyc * (here // WIDE)
    count = weights.shape[0]
    return pl.pallas_call(
        functools.partial(lens, bands, ords, cyc, npix),
        out_shape=(
            jax.ShapeDtypeStruct((3, cyc, here), jnp.bfloat16),
            jax.ShapeDtypeStruct((3, cyc, here), jnp.float32),
        ),
        in_specs=[smem, smem, vmem, anywhere],
        out_specs=(vmem, vmem),
        scratch_shapes=[
            pltpu.VMEM((lines, ords * BLK), jnp.float32),
            pltpu.VMEM((lines, ords * BLK), jnp.float32),
            pltpu.VMEM((WIDE // BLK, lines, BLK), jnp.float32),
            pltpu.VMEM((count * 4 // BLK, BLK, BLK), jnp.float32),
            pltpu.VMEM(weights.shape, jnp.bfloat16),
            pltpu.SemaphoreType.DMA((CHUNKS,)),
        ],
        compiler_params=pltpu.CompilerParams(vmem_limit_bytes=60 * 2**20),
        name="lens",
    )(src_band.reshape(count), src_block, coef, weights)


def solution(mesh):
    placed = (
        P("sim", "ord", "band"),
        P(None, "ord", "band"),
        P("ord"),
        P("band"),
        P(("sim", "band", "ord"), None),
        P(("sim", "band", "ord")),
        P(("sim", "band", "ord"), None, None),
    )

    def whole(alm, legendre, order_ids, cycle_number, src_band, src_block, weights):
        blocks = weights.shape[0] // mesh.shape["sim"]
        npix = blocks * weights.shape[2] // cycle_number.shape[0]
        return jax.shard_map(
            functools.partial(local, mesh.shape["band"], mesh.shape["ord"], npix),
            mesh=mesh,
            in_specs=placed,
            out_specs=(P("sim", "band", "ord"), P("sim", "band", "ord")),
            check_vma=False,
        )(alm, legendre, order_ids, cycle_number, src_band, src_block, weights)

    return whole
```
